256 devices in a mesh: ctx: 128 (over z, y, x), rsp: 2 (over core).
Axes of the slice: x: 4, y: 4, z: 8, core: 2. Of those that a mesh axis runs over, the one named last changes fastest.
Arguments:
- prompt_keys: bfloat16 [32768, 1024], P(('ctx', 'rsp')), may hold values from -3 to 3
- prompt_values: bfloat16 [32768, 1024], P(('ctx', 'rsp')), may hold values from -3 to 3
- block_offsets: int32 [128], replicated, may hold values from 0 to 127, each once
- prompt_queries: bfloat16 [32768, 8192], P(('ctx', 'rsp')), may hold values from -3 to 3
- prompt_cotangent: bfloat16 [32768, 8192], P(('ctx', 'rsp')), may hold values from -1.1953125 to 1.1953125
- prompt_lse: float32 [32768, 64], P(('ctx', 'rsp')), may hold values from 3 to 5
- prompt_delta: float32 [32768, 64], P(('ctx', 'rsp')), may hold values from -4 to 4
- response_queries: bfloat16 [16384, 8192], P(('ctx', 'rsp')), may hold values from -3 to 3
- response_cotangent: bfloat16 [16384, 8192], P(('ctx', 'rsp')), may hold values from -1.1953125 to 1.1953125
- response_lse: float32 [16384, 64], P(('ctx', 'rsp')), may hold values from 3 to 5
- response_delta: float32 [16384, 64], P(('ctx', 'rsp')), may hold values from -4 to 4
- response_ids: int32 [16384], P(('ctx', 'rsp')), may hold values from 0 to 15
- advantages: float32 [16], replicated, may hold values from -4 to 4
Outputs:
- response_grad: bfloat16 [16384, 8192], P(('ctx', 'rsp'))
- prompt_grad: bfloat16 [32768, 8192], P(('ctx', 'rsp'))
- key_grad: bfloat16 [32768, 1024], P(('ctx', 'rsp'))
- value_grad: bfloat16 [32768, 1024], P(('ctx', 'rsp'))
The draws below stay inside these ranges and needn't reach their ends.
All inputs are finite; a program needn't handle non-finite values.
Results may differ from the reference program's by a relative error of at most 0.0077.
Values may be sent and summed in bfloat16 or wider, within the bound.
A program may use at most 64 MiB of HBM per device.

```python
import jax
import jax.numpy as jnp
from jax import lax

HEADS = 64
KV_HEADS = 8
HEAD_DIM = 128
QW = 8192
KVW = 1024
P_SUB = 128
R_DEV = 64
RESPONSES = 16
BLOCK = 256
PROMPT = 32768
RROWS = 16384
N_CTX = 128
N_RSP = 2


def set_ends(drawn, key, low, largest):
    longest = drawn.shape.index(max(drawn.shape))
    spots = []
    for shift in (0, 1):
        where = [jax.random.randint(jax.random.fold_in(key, axis), (), 0, length) for axis, length in enumerate(drawn.shape)]
        where[longest] = (where[longest] + shift) % drawn.shape[longest]
        spots.append(tuple(where))
    return drawn.at[spots[0]].set(low).at[spots[1]].set(largest)


def block_scale(key, dims, cuts, least, top_value):
    loudness = 1.0
    for position, parts in cuts:
        draws = jax.random.uniform(jax.random.fold_in(jax.random.fold_in(key, 6), position), (parts,), jnp.float32, least / len(cuts), top_value / len(cuts))
        loudness = loudness * jnp.repeat(jnp.exp(draws), dims[position] // parts).reshape((-1,) + (1,) * (len(dims) - 1 - position))
    return loudness


def scatter_about(own_key, extent, scale, reach, cuts=(), dtype=jnp.bfloat16):
    array = jax.random.normal(own_key, extent, jnp.float32) * scale
    if len(cuts) > 0:
        array = block_scale(own_key, extent, cuts, -0.22, 0.18) * array
    return jnp.clip(array, min=-reach, max=reach).astype(dtype)


def setup_inputs(seed: int = 0) -> dict:
    key_list = jax.random.split(jax.random.key(seed), 14)
    prompt_keys = scatter_about(key_list[0], (PROMPT, KVW), 1.0, 3.0, ((0, 256),))
    prompt_values = scatter_about(key_list[1], (PROMPT, KVW), 1.0, 3.0, ((0, 256),))
    block_offsets = jax.random.permutation(key_list[2], N_CTX).astype(jnp.int32)
    prompt_queries = scatter_about(key_list[3], (PROMPT, QW), 1.0, 3.0, ((0, 256),))
    prompt_cotangent = scatter_about(key_list[4], (PROMPT, QW), 0.3, 1.1953125, ((0, 256),))
    prompt_lse = jnp.clip(3.0 + 2.0 * jax.random.uniform(key_list[5], (PROMPT, HEADS), jnp.float32) ** block_scale(key_list[5], (PROMPT, HEADS), ((0, 256),), -0.2, 0.2), 3.0, 5.0)
    prompt_delta = scatter_about(key_list[6], (PROMPT, HEADS), 1.0, 4.0, ((0, 256),), jnp.float32)
    response_queries = scatter_about(key_list[7], (RROWS, QW), 1.0, 3.0, ((0, 256),))
    response_cotangent = scatter_about(key_list[8], (RROWS, QW), 0.3, 1.1953125, ((0, 256),))
    response_lse = jnp.clip(3.0 + 2.0 * jax.random.uniform(key_list[9], (RROWS, HEADS), jnp.float32) ** block_scale(key_list[9], (RROWS, HEADS), ((0, 256),), -0.2, 0.2), 3.0, 5.0)
    response_delta = scatter_about(key_list[10], (RROWS, HEADS), 1.0, 4.0, ((0, 256),), jnp.float32)
    response_ids = set_ends(jax.random.randint(key_list[11], (RROWS,), 0, RESPONSES), jax.random.fold_in(key_list[11], 1), 0, RESPONSES - 1).astype(jnp.int32)
    advantages = scatter_about(key_list[12], (RESPONSES,), 1.0, 4.0, (), jnp.float32)
    return {"prompt_keys": prompt_keys, "prompt_values": prompt_values, "block_offsets": block_offsets, "prompt_queries": prompt_queries, "prompt_cotangent": prompt_cotangent, "prompt_lse": prompt_lse, "prompt_delta": prompt_delta, "response_queries": response_queries, "response_cotangent": response_cotangent, "response_lse": response_lse, "response_delta": response_delta, "response_ids": response_ids, "advantages": advantages}


def tile_grads(queries, cotangent, lse_rows, delta_rows, keys, values, factor):
    row_count = queries.shape[0]
    key_count = keys.shape[0]
    per_kv = HEADS // KV_HEADS
    score_scale = HEAD_DIM ** -0.5
    head_queries = queries.astype(jnp.float32).reshape(row_count, KV_HEADS, per_kv, HEAD_DIM)
    cotangent_head_rows = cotangent.astype(jnp.float32).reshape(row_count, KV_HEADS, per_kv, HEAD_DIM)
    head_keys = keys.astype(jnp.float32).reshape(key_count, KV_HEADS, HEAD_DIM)
    head_values = values.astype(jnp.float32).reshape(key_count, KV_HEADS, HEAD_DIM)
    logit_scores = jnp.einsum("xnoh,snh->xnos", head_queries, head_keys) * score_scale
    softmax_rows = jnp.exp(logit_scores - lse_rows.reshape(row_count, KV_HEADS, per_kv)[..., None]) * factor
    lowered_rows = lax.optimization_barrier(softmax_rows.astype(jnp.bfloat16)).astype(jnp.float32)
    value_gradient = jnp.einsum("mios,mioz->siz", lowered_rows, cotangent_head_rows)
    probability_gradient = jnp.einsum("xnoh,snh->xnos", cotangent_head_rows, head_values)
    grad_score = softmax_rows * (probability_gradient - delta_rows.reshape(row_count, KV_HEADS, per_kv)[..., None])
    lowered_score = lax.optimization_barrier(grad_score.astype(jnp.bfloat16)).astype(jnp.float32)
    key_gradient = jnp.einsum("mios,mioz->siz", lowered_score, head_queries) * score_scale
    query_gradient = jnp.einsum("qxof,fxm->qxom", lowered_score, head_keys) * score_scale
    return (query_gradient.reshape(row_count, HEADS * HEAD_DIM),
            key_gradient.reshape(key_count, KV_HEADS * HEAD_DIM),
            value_gradient.reshape(key_count, KV_HEADS * HEAD_DIM))


def reference(prompt_keys, prompt_values, block_offsets, prompt_queries, prompt_cotangent, prompt_lse, prompt_delta,
              response_queries, response_cotangent, response_lse, response_delta, response_ids, advantages):
    weight = advantages[response_ids]
    weighted = (weight[:, None] * response_cotangent.astype(jnp.float32)).astype(jnp.bfloat16)
    weighted_delta = weight[:, None] * response_delta
    key_blocks = prompt_keys.reshape(N_CTX, BLOCK, KVW)
    value_blocks = prompt_values.reshape(N_CTX, BLOCK, KVW)
    keys_in = jnp.roll(key_blocks, 1, axis=0)
    values_in = jnp.roll(value_blocks, 1, axis=0)
    offsets_in = jnp.roll(block_offsets, 1)
    visible = jnp.where(offsets_in < block_offsets, 1.0, 0.0).astype(jnp.float32)
    prompt_q = prompt_queries.reshape(N_CTX, N_RSP, P_SUB, QW)
    prompt_c = prompt_cotangent.reshape(N_CTX, N_RSP, P_SUB, QW)
    prompt_l = prompt_lse.reshape(N_CTX, N_RSP, P_SUB, HEADS)
    prompt_d = prompt_delta.reshape(N_CTX, N_RSP, P_SUB, HEADS)
    answer_q = response_queries.reshape(N_CTX, N_RSP, R_DEV, QW)
    answer_c = weighted.reshape(N_CTX, N_RSP, R_DEV, QW)
    answer_l = response_lse.reshape(N_CTX, N_RSP, R_DEV, HEADS)
    answer_d = weighted_delta.reshape(N_CTX, N_RSP, R_DEV, HEADS)

    def one_block(pieces):
        keys, values, seen, pq_rows, pc_rows, pl_rows, pd_rows, aq_rows, ac_rows, al_rows, ad_rows = pieces

        def one_group(group_pieces):
            pq_one, pc_one, pl_one, pd_one, aq_one, ac_one, al_one, ad_one = group_pieces
            answer_dq, answer_dk, answer_dv = tile_grads(aq_one, ac_one, al_one, ad_one, keys, values, jnp.float32(1.0))
            prompt_dq, prompt_dk, prompt_dv = tile_grads(pq_one, pc_one, pl_one, pd_one, keys, values, seen)
            partials = jnp.stack((answer_dk + prompt_dk, answer_dv + prompt_dv)).astype(jnp.bfloat16)
            return answer_dq.astype(jnp.bfloat16), prompt_dq.astype(jnp.bfloat16), partials

        answer_dq, prompt_dq, partials = lax.map(one_group, (pq_rows, pc_rows, pl_rows, pd_rows, aq_rows, ac_rows, al_rows, ad_rows))
        partials = lax.optimization_barrier(partials)
        summed = jnp.sum(partials.astype(jnp.float32), axis=0).astype(jnp.bfloat16)
        return answer_dq, prompt_dq, summed

    answer_dq, prompt_dq, summed = lax.map(one_block, (keys_in, values_in, visible, prompt_q, prompt_c, prompt_l, prompt_d,
                                                       answer_q, answer_c, answer_l, answer_d))
    summed = jnp.roll(summed, -1, axis=0)
    key_grad = summed[:, 0].reshape(PROMPT, KVW)
    value_grad = summed[:, 1].reshape(PROMPT, KVW)
    return answer_dq.reshape(RROWS, QW), prompt_dq.reshape(PROMPT, QW), key_grad, value_grad
```

```python
import jax
import jax.numpy as jnp
from jax import lax
from jax.experimental import pallas as pl
from jax.experimental.pallas import tpu as pltpu
from jax.sharding import PartitionSpec as P

HEADS = 64
KV = 8
PER = HEADS // KV
DIM = 128
RESPONSES = 16
PROWS = 128
RROWS = 64
KEYS = 256
TILES = 6
SCALE = float(DIM**-0.5)
LOG2E = 1.4426950408889634
SCALE2 = SCALE * LOG2E
HIDDEN = 1e30
F32 = jnp.float32
BF16 = jnp.bfloat16
MESH = pl.DeviceIdType.MESH


def dot(a, b, ca, cb):
    return lax.dot_general(a, b, (((ca,), (cb,)), ((), ())), preferred_element_type=F32)


def kernel(
    pk, pv, offsets, pq, pc, plse, pdel, rq, rc, rlse, rdel, ids, adv,
    rgrad, pgrad, kvgrad,
    kvin, q_p, c_p, q_r, c_r, w_r,
    lp, ep, lr, er, lse_p, del_p, lse_r, del_r, ids_v, offsets_s, adv_s, square,
    probs, score_a, score_b, part, got, back,
    load_sem, small_sem, kv_send, kv_recv, fw_send, fw_recv,
    ex_send, ex_recv, back_send, back_recv,
):
    count = lax.axis_size("ctx")
    me = lax.axis_index("ctx")
    core = lax.axis_index("rsp")
    right = lax.rem(me + 1, count)
    left = lax.rem(me + count - 1, count)
    other = 1 - core
    mine = pl.ds(pl.multiple_of(core * PROWS, PROWS), PROWS)
    theirs = pl.ds(pl.multiple_of(other * PROWS, PROWS), PROWS)

    barrier = pltpu.get_barrier_semaphore()
    for device in ((left, core), (me, other)):
        pl.semaphore_signal(barrier, inc=1, device_id=device, device_id_type=MESH)

    small = [
        pltpu.make_async_copy(source, target, small_sem.at[i])
        for i, (source, target) in enumerate(
            (
                (ids, ids_v), (plse, lse_p), (pdel, del_p), (rlse, lse_r),
                (rdel, del_r), (offsets, offsets_s), (adv, adv_s),
            )
        )
    ]
    loads = [
        pltpu.make_async_copy(source, target, load_sem.at[i])
        for i, (source, target) in enumerate(((rc, c_r), (pq, q_p), (pc, c_p), (rq, q_r)))
    ]
    for copy in small:
        copy.start()

    def send_kv(n):
        columns = pl.ds(pl.multiple_of(n * DIM, DIM), DIM)
        return [
            pltpu.make_async_remote_copy(
                src_ref=source.at[:, columns],
                dst_ref=kvin.at[n, i, mine, :],
                send_sem=kv_send.at[i, n],
                recv_sem=kv_recv.at[i, n],
                device_id=(right, core),
                device_id_type=MESH,
            )
            for i, source in enumerate((pk, pv))
        ]

    def kv_arrived(n):
        for copy in send_kv(n):
            copy.wait_recv()

    def forward(n):
        return pltpu.make_async_remote_copy(
            src_ref=kvin.at[n, :, mine, :],
            dst_ref=kvin.at[n, :, mine, :],
            send_sem=fw_send.at[n],
            recv_sem=fw_recv.at[n],
            device_id=(me, other),
            device_id_type=MESH,
        )

    def exchange(n):
        return pltpu.make_async_remote_copy(
            src_ref=part.at[n, :, theirs, :],
            dst_ref=got.at[n],
            send_sem=ex_send.at[n],
            recv_sem=ex_recv.at[n],
            device_id=(me, other),
            device_id_type=MESH,
        )

    def give_back(n):
        return pltpu.make_async_remote_copy(
            src_ref=back.at[n],
            dst_ref=kvgrad.at[:, :, pl.ds(pl.multiple_of(n * DIM, DIM), DIM)],
            send_sem=back_send.at[n],
            recv_sem=back_recv.at[n],
            device_id=(left, core),
            device_id_type=MESH,
        )

    pl.semaphore_wait(barrier, 2)
    for n in range(KV):
        for copy in send_kv(n):
            copy.start()
    for copy in loads:
        copy.start()

    for copy in small:
        copy.wait()
    visible = offsets_s[left] < offsets_s[me]
    weight_row = jnp.zeros((1, RROWS), F32)
    for j in range(RESPONSES):
        weight_row = weight_row + jnp.where(ids_v[...] == j, adv_s[j], 0.0)
    square[...] = jnp.zeros_like(square)
    square[:, 0:RROWS] = jnp.broadcast_to(weight_row, (PROWS, RROWS))
    weight = square[...].T[0:RROWS, :]

    def turned(top, bottom):
        square[0:RROWS, 0:HEADS] = top
        square[RROWS:PROWS, 0:HEADS] = bottom
        return square[...].T

    def turned_response(values):
        return turned(values, jnp.concatenate((values[:, 4:], values[:, :4]), axis=1))

    lse_t = jnp.where(visible, lse_p[...] * LOG2E, HIDDEN)
    del_t = del_p[...]
    rlse_t = turned_response(lse_r[...]) * LOG2E
    rdel_t = turned_response(del_r[...] * weight[:, 0:HEADS])
    for n in range(KV):
        lp[n] = lse_t[n * PER : (n + 1) * PER]
        ep[n] = del_t[n * PER : (n + 1) * PER]
        lr[n] = rlse_t[n * PER : (n + 1) * PER]
        er[n] = rdel_t[n * PER : (n + 1) * PER]

    for copy in loads:
        copy.wait()

    def weigh(i, carry):
        columns = pl.ds(pl.multiple_of(i * DIM, DIM), DIM)
        w_r[:, columns] = (weight * c_r[:, columns].astype(F32)).astype(BF16)
        return carry

    lax.fori_loop(0, HEADS, weigh, 0)

    def spans(n, t):
        if t < 4:
            heads = (2 * t, 2 * t + 1)
        else:
            u = (t - 4) * 2
            heads = (u, u + 4, u + 1, u + 5)
        return [pl.ds(pl.multiple_of(n * PER * DIM + h * DIM, DIM), DIM) for h in heads]

    def rows_of(n, t, prompt, response):
        source = prompt if t < 4 else response
        return jnp.concatenate([source[:, columns] for columns in spans(n, t)], axis=0)

    def stats_of(n, t, prompt, response):
        source, first = (prompt, 2 * t) if t < 4 else (response, (t - 4) * 2)
        return jnp.concatenate((source[n, first : first + 1, :], source[n, first + 1 : first + 2, :]), axis=1)

    def scores(n, t, score):
        span = pl.ds(t * KEYS, KEYS)
        st = dot(kvin[n, 0], rows_of(n, t, q_p, q_r), 1, 1)
        gt = dot(kvin[n, 1], rows_of(n, t, c_p, w_r), 1, 1)
        p = jnp.exp2(st * SCALE2 - stats_of(n, t, lp, lr))
        probs[:, span] = p.astype(BF16)
        score[:, span] = (p * (gt - stats_of(n, t, ep, er))).astype(BF16)

    def query_grads(n, t, score):
        grad = dot(kvin[n, 0].T, score[:, pl.ds(t * KEYS, KEYS)], 1, 0)
        grad = (grad.T * SCALE).astype(BF16)
        target, rows = (pgrad, PROWS) if t < 4 else (rgrad, RROWS)
        for i, columns in enumerate(spans(n, t)):
            target[:, columns] = grad[i * rows : (i + 1) * rows]

    def key_grads(n, score):
        queries = jnp.concatenate([rows_of(n, t, q_p, q_r) for t in range(TILES)], axis=0)
        cotangent = jnp.concatenate([rows_of(n, t, c_p, w_r) for t in range(TILES)], axis=0)
        part[n, 1] = dot(probs[...], cotangent, 1, 0).astype(BF16)
        part[n, 0] = (dot(score[...], queries, 1, 0) * SCALE).astype(BF16)

    def send_sum(n):
        exchange(n).wait_recv()
        back[n] = (part[n, :, mine, :].astype(F32) + got[n].astype(F32)).astype(BF16)
        give_back(n).start()

    def step(n, score, before, first=False, last=False):
        if not (first or last):
            kv_arrived(n + 1)
            forward(n + 1).start()
        forward(n).wait_recv()
        for t in range(TILES):
            if first and t == TILES // 2:
                kv_arrived(n + 1)
                forward(n + 1).start()
            scores(n, t, score)
            if not first:
                query_grads(n - 1, t, before)
        key_grads(n, score)
        exchange(n).start()
        if not first:
            send_sum(n - 1)

    kv_arrived(0)
    forward(0).start()
    step(0, score_a, score_b, first=True)

    def pair(m, carry):
        step(2 * m + 1, score_b, score_a)
        step(2 * m + 2, score_a, score_b)
        return carry

    lax.fori_loop(0, (KV - 2) // 2, pair, 0)
    step(KV - 1, score_b, score_a, last=True)
    for t in range(TILES):
        query_grads(KV - 1, t, score_b)
    send_sum(KV - 1)

    def finish(n, carry):
        for copy in send_kv(n):
            copy.wait_send()
        forward(n).wait_send()
        exchange(n).wait_send()
        give_back(n).wait()
        return carry

    lax.fori_loop(0, KV, finish, 0)


def write_out(rgrad, pgrad, kvgrad, rgrad_out, pgrad_out, kgrad_out, vgrad_out, sems):
    copies = [
        pltpu.make_async_copy(source, target, sems.at[i])
        for i, (source, target) in enumerate(
            (
                (pgrad, pgrad_out), (rgrad, rgrad_out),
                (kvgrad.at[0], kgrad_out), (kvgrad.at[1], vgrad_out),
            )
        )
    ]
    for copy in copies:
        copy.start()
    for copy in copies:
        copy.wait()


def body(pk, pv, offsets, pq, pc, plse, pdel, rq, rc, rlse, rdel, ids, adv):
    main = pl.BlockSpec(memory_space=pltpu.HBM)
    vector = pl.BlockSpec(memory_space=pltpu.VMEM)
    wide = HEADS * DIM
    operands = (pk, pv, offsets, pq, pc, plse.T, pdel.T, rq, rc, rlse, rdel, ids.reshape(1, RROWS), adv)
    operands = [pltpu.with_memory_space_constraint(x, pltpu.HBM) for x in operands]
    rgrad, pgrad, kvgrad = pl.pallas_call(
        kernel,
        out_shape=(
            pltpu.VMEM((RROWS, wide), BF16),
            pltpu.VMEM((PROWS, wide), BF16),
            pltpu.VMEM((2, PROWS, KV * DIM), BF16),
        ),
        in_specs=[main] * 13,
        out_specs=(vector, vector, vector),
        scratch_shapes=[
            pltpu.VMEM((KV, 2, KEYS, DIM), BF16),
            pltpu.VMEM((PROWS, wide), BF16),
            pltpu.VMEM((PROWS, wide), BF16),
            pltpu.VMEM((RROWS, wide), BF16),
            pltpu.VMEM((RROWS, wide), BF16),
            pltpu.VMEM((RROWS, wide), BF16),
            pltpu.VMEM((KV, PER, PROWS), F32),
            pltpu.VMEM((KV, PER, PROWS), F32),
            pltpu.VMEM((KV, PER, PROWS), F32),
            pltpu.VMEM((KV, PER, PROWS), F32),
            pltpu.VMEM((HEADS, PROWS), F32),
            pltpu.VMEM((HEADS, PROWS), F32),
            pltpu.VMEM((RROWS, HEADS), F32),
            pltpu.VMEM((RROWS, HEADS), F32),
            pltpu.VMEM((1, RROWS), jnp.int32),
            pltpu.SMEM(offsets.shape, jnp.int32),
            pltpu.SMEM((RESPONSES,), F32),
            pltpu.VMEM((PROWS, PROWS), F32),
            pltpu.VMEM((KEYS, TILES * KEYS), BF16),
            pltpu.VMEM((KEYS, TILES * KEYS), BF16),
            pltpu.VMEM((KEYS, TILES * KEYS), BF16),
            pltpu.VMEM((KV, 2, KEYS, DIM), BF16),
            pltpu.VMEM((KV, 2, PROWS, DIM), BF16),
            pltpu.VMEM((KV, 2, PROWS, DIM), BF16),
            pltpu.SemaphoreType.DMA((4,)),
            pltpu.SemaphoreType.DMA((7,)),
            pltpu.SemaphoreType.DMA((2, KV)),
            pltpu.SemaphoreType.DMA((2, KV)),
            pltpu.SemaphoreType.DMA((KV,)),
            pltpu.SemaphoreType.DMA((KV,)),
            pltpu.SemaphoreType.DMA((KV,)),
            pltpu.SemaphoreType.DMA((KV,)),
            pltpu.SemaphoreType.DMA((KV,)),
            pltpu.SemaphoreType.DMA((KV,)),
        ],
        compiler_params=pltpu.CompilerParams(
            collective_id=0, has_side_effects=True, vmem_limit_bytes=28 * 2**20
        ),
        name="prefix_backward",
    )(*operands)
    grads = [pltpu.with_memory_space_constraint(x, pltpu.VMEM) for x in (rgrad, pgrad, kvgrad)]
    return pl.pallas_call(
        write_out,
        out_shape=(
            jax.ShapeDtypeStruct((RROWS, wide), BF16),
            jax.ShapeDtypeStruct((PROWS, wide), BF16),
            jax.ShapeDtypeStruct((PROWS, KV * DIM), BF16),
            jax.ShapeDtypeStruct((PROWS, KV * DIM), BF16),
        ),
        in_specs=[vector] * 3,
        out_specs=(main, main, main, main),
        scratch_shapes=[pltpu.SemaphoreType.DMA((4,))],
        compiler_params=pltpu.CompilerParams(vmem_limit_bytes=4 * 2**20),
        name="write_out",
    )(*grads)


def solution(mesh):
    rows = P(("ctx", "rsp"), None)
    return jax.shard_map(
        body,
        mesh=mesh,
        in_specs=(rows, rows, P(), rows, rows, rows, rows, rows, rows, rows, rows, P(("ctx", "rsp")), P()),
        out_specs=(rows, rows, rows, rows),
        check_vma=False,
    )
```

```python
import jax
import jax.numpy as jnp
from jax import lax
from jax.experimental import pallas as pl
from jax.experimental.pallas import tpu as pltpu
from jax.sharding import PartitionSpec as P

HEADS = 64
KV = 8
PER = HEADS // KV
DIM = 128
RESPONSES = 16
PROWS = 128
RROWS = 64
KEYS = 256
TILES = 6
SCALE = float(DIM**-0.5)
LOG2E = 1.4426950408889634
SCALE2 = SCALE * LOG2E
HIDDEN = 1e30
F32 = jnp.float32
BF16 = jnp.bfloat16
MESH = pl.DeviceIdType.MESH


def dot(a, b, ca, cb):
    return lax.dot_general(a, b, (((ca,), (cb,)), ((), ())), preferred_element_type=F32)


def kernel(
    pk, pv, offsets, pq, pc, plse, pdel, rq, rc, rlse, rdel, ids, adv,
    rgrad, pgrad, kvgrad,
    kvin, q_p, c_p, q_r, c_r, w_r,
    lp, ep, lr, er, lse_p, del_p, lse_r, del_r, ids_v, offsets_s, adv_s, square,
    probs, score_a, score_b, part, got, back, final, final_got,
    load_sem, small_sem, kv_send, kv_recv, fw_send, fw_recv,
    ex_send, ex_recv, back_send, back_recv, last_send,
):
    count = lax.axis_size("ctx")
    me = lax.axis_index("ctx")
    core = lax.axis_index("rsp")
    right = lax.rem(me + 1, count)
    left = lax.rem(me + count - 1, count)
    other = 1 - core
    mine = pl.ds(pl.multiple_of(core * PROWS, PROWS), PROWS)
    theirs = pl.ds(pl.multiple_of(other * PROWS, PROWS), PROWS)

    barrier = pltpu.get_barrier_semaphore()
    for device in ((left, core), (me, other)):
        pl.semaphore_signal(barrier, inc=1, device_id=device, device_id_type=MESH)

    small = [
        pltpu.make_async_copy(source, target, small_sem.at[i])
        for i, (source, target) in enumerate(
            (
                (ids, ids_v), (plse, lse_p), (pdel, del_p), (rlse, lse_r),
                (rdel, del_r), (offsets, offsets_s), (adv, adv_s),
            )
        )
    ]
    loads = [
        pltpu.make_async_copy(source, target, load_sem.at[i])
        for i, (source, target) in enumerate(((rc, c_r), (pq, q_p), (pc, c_p), (rq, q_r)))
    ]
    for copy in small:
        copy.start()

    def send_kv(n):
        columns = pl.ds(pl.multiple_of(n * DIM, DIM), DIM)
        return [
            pltpu.make_async_remote_copy(
                src_ref=source.at[:, columns],
                dst_ref=kvin.at[n, i, mine, :],
                send_sem=kv_send.at[i, n],
                recv_sem=kv_recv.at[i, n],
                device_id=(right, core),
                device_id_type=MESH,
            )
            for i, source in enumerate((pk, pv))
        ]

    def kv_arrived(n):
        for copy in send_kv(n):
            copy.wait_recv()

    def forward(n):
        return pltpu.make_async_remote_copy(
            src_ref=kvin.at[n, :, mine, :],
            dst_ref=kvin.at[n, :, mine, :],
            send_sem=fw_send.at[n],
            recv_sem=fw_recv.at[n],
            device_id=(me, other),
            device_id_type=MESH,
        )

    def exchange(n):
        return pltpu.make_async_remote_copy(
            src_ref=part.at[n, :, theirs, :],
            dst_ref=got.at[n],
            send_sem=ex_send.at[n],
            recv_sem=ex_recv.at[n],
            device_id=(me, other),
            device_id_type=MESH,
        )

    def hand_over():
        return pltpu.make_async_remote_copy(
            src_ref=part.at[KV - 1],
            dst_ref=final_got,
            send_sem=ex_send.at[KV - 1],
            recv_sem=ex_recv.at[KV - 1],
            device_id=(me, 0),
            device_id_type=MESH,
        )

    def give_last(target):
        return pltpu.make_async_remote_copy(
            src_ref=final.at[:, pl.ds(target * PROWS, PROWS), :],
            dst_ref=kvgrad.at[:, :, pl.ds((KV - 1) * DIM, DIM)],
            send_sem=last_send.at[target],
            recv_sem=back_recv.at[KV - 1],
            device_id=(left, target),
            device_id_type=MESH,
        )

    def give_back(n):
        return pltpu.make_async_remote_copy(
            src_ref=back.at[n],
            dst_ref=kvgrad.at[:, :, pl.ds(pl.multiple_of(n * DIM, DIM), DIM)],
            send_sem=back_send.at[n],
            recv_sem=back_recv.at[n],
            device_id=(left, core),
            device_id_type=MESH,
        )

    pl.semaphore_wait(barrier, 2)
    for n in range(KV):
        for copy in send_kv(n):
            copy.start()
    for copy in loads:
        copy.start()

    for copy in small:
        copy.wait()
    visible = offsets_s[left] < offsets_s[me]
    weight_row = jnp.zeros((1, RROWS), F32)
    for j in range(RESPONSES):
        weight_row = weight_row + jnp.where(ids_v[...] == j, adv_s[j], 0.0)
    square[...] = jnp.zeros_like(square)
    square[:, 0:RROWS] = jnp.broadcast_to(weight_row, (PROWS, RROWS))
    weight = square[...].T[0:RROWS, :]

    def turned(top, bottom):
        square[0:RROWS, 0:HEADS] = top
        square[RROWS:PROWS, 0:HEADS] = bottom
        return square[...].T

    def turned_response(values):
        return turned(values, jnp.concatenate((values[:, 4:], values[:, :4]), axis=1))

    lse_t = jnp.where(visible, lse_p[...] * LOG2E, HIDDEN)
    del_t = del_p[...]
    rlse_t = turned_response(lse_r[...]) * LOG2E
    rdel_t = turned_response(del_r[...] * weight[:, 0:HEADS])
    for n in range(KV):
        lp[n] = lse_t[n * PER : (n + 1) * PER]
        ep[n] = del_t[n * PER : (n + 1) * PER]
        lr[n] = rlse_t[n * PER : (n + 1) * PER]
        er[n] = rdel_t[n * PER : (n + 1) * PER]

    for copy in loads:
        copy.wait()

    def weigh(i, carry):
        columns = pl.ds(pl.multiple_of(i * DIM, DIM), DIM)
        w_r[:, columns] = (weight * c_r[:, columns].astype(F32)).astype(BF16)
        return carry

    lax.fori_loop(0, HEADS, weigh, 0)

    def spans(n, t):
        if t < 4:
            heads = (2 * t, 2 * t + 1)
        else:
            u = (t - 4) * 2
            heads = (u, u + 4, u + 1, u + 5)
        return [pl.ds(pl.multiple_of(n * PER * DIM + h * DIM, DIM), DIM) for h in heads]

    def rows_of(n, t, prompt, response):
        source = prompt if t < 4 else response
        return jnp.concatenate([source[:, columns] for columns in spans(n, t)], axis=0)

    def stats_of(n, t, prompt, response):
        source, first = (prompt, 2 * t) if t < 4 else (response, (t - 4) * 2)
        return jnp.concatenate((source[n, first : first + 1, :], source[n, first + 1 : first + 2, :]), axis=1)

    def scores(n, t, score):
        span = pl.ds(t * KEYS, KEYS)
        st = dot(kvin[n, 0], rows_of(n, t, q_p, q_r), 1, 1)
        gt = dot(kvin[n, 1], rows_of(n, t, c_p, w_r), 1, 1)
        p = jnp.exp2(st * SCALE2 - stats_of(n, t, lp, lr))
        probs[:, span] = p.astype(BF16)
        score[:, span] = (p * (gt - stats_of(n, t, ep, er))).astype(BF16)

    def query_grads(n, t, score):
        grad = dot(kvin[n, 0].T, score[:, pl.ds(t * KEYS, KEYS)], 1, 0)
        grad = (grad * SCALE).astype(BF16).T
        target, rows = (pgrad, PROWS) if t < 4 else (rgrad, RROWS)
        for i, columns in enumerate(spans(n, t)):
            target[:, columns] = grad[i * rows : (i + 1) * rows]

    def value_grads(n):
        cotangent = jnp.concatenate([rows_of(n, t, c_p, w_r) for t in range(TILES)], axis=0)
        part[n, 1] = dot(probs[...], cotangent, 1, 0).astype(BF16)

    def key_grads(n, score):
        queries = jnp.concatenate([rows_of(n, t, q_p, q_r) for t in range(TILES)], axis=0)
        part[n, 0] = (dot(score[...], queries, 1, 0) * SCALE).astype(BF16)

    def send_sum(n):
        exchange(n).wait_recv()
        back[n] = (part[n, :, mine, :].astype(F32) + got[n].astype(F32)).astype(BF16)
        give_back(n).start()

    def step(n, score, before, first=False, last=False):
        if not (first or last):
            kv_arrived(n + 1)
            forward(n + 1).start()
        forward(n).wait_recv()
        for t in range(TILES):
            if first and t == TILES // 2:
                kv_arrived(n + 1)
                forward(n + 1).start()
            scores(n, t, score)
            if not first:
                query_grads(n - 1, t, before)
        value_grads(n)
        key_grads(n, score)
        if not last:
            exchange(n).start()
        if not first:
            send_sum(n - 1)

    kv_arrived(0)
    forward(0).start()
    step(0, score_a, score_b, first=True)

    def pair(m, carry):
        step(2 * m + 1, score_b, score_a)
        step(2 * m + 2, score_a, score_b)
        return carry

    lax.fori_loop(0, (KV - 2) // 2, pair, 0)
    step(KV - 1, score_b, score_a, last=True)

    @pl.when(core == 1)
    def _():
        hand_over().start()

    for t in range(TILES):
        query_grads(KV - 1, t, score_b)

    @pl.when(core == 0)
    def _():
        hand_over().wait_recv()
        final[...] = (part[KV - 1].astype(F32) + final_got[...].astype(F32)).astype(BF16)
        for target in range(2):
            give_last(target).start()

    def finish(n, carry):
        for copy in send_kv(n):
            copy.wait_send()
        forward(n).wait_send()

        @pl.when(n < KV - 1)
        def _():
            exchange(n).wait_send()
            give_back(n).wait()

        return carry

    lax.fori_loop(0, KV, finish, 0)

    @pl.when(core == 1)
    def _():
        hand_over().wait_send()

    @pl.when(core == 0)
    def _():
        for target in range(2):
            give_last(target).wait_send()

    give_last(0).wait_recv()


def write_out(rgrad, pgrad, kvgrad, rgrad_out, pgrad_out, kgrad_out, vgrad_out, sems):
    copies = [
        pltpu.make_async_copy(source, target, sems.at[i])
        for i, (source, target) in enumerate(
            (
                (pgrad, pgrad_out), (rgrad, rgrad_out),
                (kvgrad.at[0], kgrad_out), (kvgrad.at[1], vgrad_out),
            )
        )
    ]
    for copy in copies:
        copy.start()
    for copy in copies:
        copy.wait()


def body(pk, pv, offsets, pq, pc, plse, pdel, rq, rc, rlse, rdel, ids, adv):
    main = pl.BlockSpec(memory_space=pltpu.HBM)
    vector = pl.BlockSpec(memory_space=pltpu.VMEM)
    wide = HEADS * DIM
    operands = (pk, pv, offsets, pq, pc, plse.T, pdel.T, rq, rc, rlse, rdel, ids.reshape(1, RROWS), adv)
    operands = [pltpu.with_memory_space_constraint(x, pltpu.HBM) for x in operands]
    rgrad, pgrad, kvgrad = pl.pallas_call(
        kernel,
        out_shape=(
            pltpu.VMEM((RROWS, wide), BF16),
            pltpu.VMEM((PROWS, wide), BF16),
            pltpu.VMEM((2, PROWS, KV * DIM), BF16),
        ),
        in_specs=[main] * 13,
        out_specs=(vector, vector, vector),
        scratch_shapes=[
            pltpu.VMEM((KV, 2, KEYS, DIM), BF16),
            pltpu.VMEM((PROWS, wide), BF16),
            pltpu.VMEM((PROWS, wide), BF16),
            pltpu.VMEM((RROWS, wide), BF16),
            pltpu.VMEM((RROWS, wide), BF16),
            pltpu.VMEM((RROWS, wide), BF16),
            pltpu.VMEM((KV, PER, PROWS), F32),
            pltpu.VMEM((KV, PER, PROWS), F32),
            pltpu.VMEM((KV, PER, PROWS), F32),
            pltpu.VMEM((KV, PER, PROWS), F32),
            pltpu.VMEM((HEADS, PROWS), F32),
            pltpu.VMEM((HEADS, PROWS), F32),
            pltpu.VMEM((RROWS, HEADS), F32),
            pltpu.VMEM((RROWS, HEADS), F32),
            pltpu.VMEM((1, RROWS), jnp.int32),
            pltpu.SMEM(offsets.shape, jnp.int32),
            pltpu.SMEM((RESPONSES,), F32),
            pltpu.VMEM((PROWS, PROWS), F32),
            pltpu.VMEM((KEYS, TILES * KEYS), BF16),
            pltpu.VMEM((KEYS, TILES * KEYS), BF16),
            pltpu.VMEM((KEYS, TILES * KEYS), BF16),
            pltpu.VMEM((KV, 2, KEYS, DIM), BF16),
            pltpu.VMEM((KV, 2, PROWS, DIM), BF16),
            pltpu.VMEM((KV, 2, PROWS, DIM), BF16),
            pltpu.VMEM((2, KEYS, DIM), BF16),
            pltpu.VMEM((2, KEYS, DIM), BF16),
            pltpu.SemaphoreType.DMA((4,)),
            pltpu.SemaphoreType.DMA((7,)),
            pltpu.SemaphoreType.DMA((2, KV)),
            pltpu.SemaphoreType.DMA((2, KV)),
            pltpu.SemaphoreType.DMA((KV,)),
            pltpu.SemaphoreType.DMA((KV,)),
            pltpu.SemaphoreType.DMA((KV,)),
            pltpu.SemaphoreType.DMA((KV,)),
            pltpu.SemaphoreType.DMA((KV,)),
            pltpu.SemaphoreType.DMA((KV,)),
            pltpu.SemaphoreType.DMA((2,)),
        ],
        compiler_params=pltpu.CompilerParams(
            collective_id=0, has_side_effects=True, vmem_limit_bytes=28 * 2**20
        ),
        name="prefix_backward",
    )(*operands)
    grads = [pltpu.with_memory_space_constraint(x, pltpu.VMEM) for x in (rgrad, pgrad, kvgrad)]
    return pl.pallas_call(
        write_out,
        out_shape=(
            jax.ShapeDtypeStruct((RROWS, wide), BF16),
            jax.ShapeDtypeStruct((PROWS, wide), BF16),
            jax.ShapeDtypeStruct((PROWS, KV * DIM), BF16),
            jax.ShapeDtypeStruct((PROWS, KV * DIM), BF16),
        ),
        in_specs=[vector] * 3,
        out_specs=(main, main, main, main),
        scratch_shapes=[pltpu.SemaphoreType.DMA((4,))],
        compiler_params=pltpu.CompilerParams(vmem_limit_bytes=4 * 2**20),
        name="write_out",
    )(*grads)


def solution(mesh):
    rows = P(("ctx", "rsp"), None)
    return jax.shard_map(
        body,
        mesh=mesh,
        in_specs=(rows, rows, P(), rows, rows, rows, rows, rows, rows, rows, rows, P(("ctx", "rsp")), P()),
        out_specs=(rows, rows, rows, rows),
        check_vma=False,
    )
```

```python
import jax
import jax.numpy as jnp
from jax import lax
from jax.experimental import pallas as pl
from jax.experimental.pallas import tpu as pltpu
from jax.sharding import PartitionSpec as P

HEADS = 64
KV = 8
PER = HEADS // KV
LATE = KV - 2
LAST = KV - 1
DIM = 128
RESPONSES = 16
PROWS = 128
RROWS = 64
KEYS = 256
TILES = 6
SCALE = float(DIM**-0.5)
LOG2E = 1.4426950408889634
SCALE2 = SCALE * LOG2E
HIDDEN = 1e30
F32 = jnp.float32
BF16 = jnp.bfloat16
MESH = pl.DeviceIdType.MESH


def dot(a, b, ca, cb):
    return lax.dot_general(a, b, (((ca,), (cb,)), ((), ())), preferred_element_type=F32)


def kernel(
    pk, pv, offsets, pq, pc, plse, pdel, rq, rc, rlse, rdel, ids, adv,
    rgrad, pgrad, kvgrad,
    kvsrc, kvin, q_p, c_p, q_r, c_r, w_r,
    lp, ep, lr, er, lse_p, del_p, lse_r, del_r, ids_v, offsets_s, adv_s, square,
    probs, score_a, score_b, part, got, back, final, final_got,
    first_send, stage_sem, load_sem, small_sem, kv_send, kv_recv, fw_send, fw_recv,
    ex_send, ex_recv, back_send, back_recv, last_send,
):
    count = lax.axis_size("ctx")
    me = lax.axis_index("ctx")
    core = lax.axis_index("rsp")
    right = lax.rem(me + 1, count)
    left = lax.rem(me + count - 1, count)
    other = 1 - core
    lead = (count - 1 - me) // (count - 1)
    tail = me // (count - 1)
    chosen = 1 - lead
    late_from = KV - 1 - lead
    mine = pl.ds(pl.multiple_of(core * PROWS, PROWS), PROWS)
    theirs = pl.ds(pl.multiple_of(other * PROWS, PROWS), PROWS)

    barrier = pltpu.get_barrier_semaphore()
    for device in ((left, core), (me, other)):
        pl.semaphore_signal(barrier, inc=1, device_id=device, device_id_type=MESH)

    small = [
        pltpu.make_async_copy(source, target, small_sem.at[i])
        for i, (source, target) in enumerate(
            (
                (ids, ids_v), (plse, lse_p), (pdel, del_p), (rlse, lse_r),
                (rdel, del_r), (offsets, offsets_s), (adv, adv_s),
            )
        )
    ]
    loads = [
        pltpu.make_async_copy(source, target, load_sem.at[i])
        for i, (source, target) in enumerate(((rc, c_r), (pq, q_p), (pc, c_p), (rq, q_r)))
    ]
    stage = [pltpu.make_async_copy(source, kvsrc.at[i], stage_sem.at[i]) for i, source in enumerate((pk, pv))]
    for copy in stage + small:
        copy.start()

    def send_kv(n):
        return pltpu.make_async_remote_copy(
            src_ref=kvsrc.at[:, :, pl.ds(pl.multiple_of(n * DIM, DIM), DIM)],
            dst_ref=kvin.at[n, :, mine, :],
            send_sem=kv_send.at[n],
            recv_sem=kv_recv.at[n],
            device_id=(right, core),
            device_id_type=MESH,
        )

    first_kv = [
        pltpu.make_async_remote_copy(
            src_ref=source.at[:, pl.ds(0, DIM)],
            dst_ref=kvin.at[0, i, mine, :],
            send_sem=first_send.at[i],
            recv_sem=kv_recv.at[0],
            device_id=(right, core),
            device_id_type=MESH,
        )
        for i, source in enumerate((pk, pv))
    ]

    def forward(n):
        return pltpu.make_async_remote_copy(
            src_ref=kvin.at[n, :, mine, :],
            dst_ref=kvin.at[n, :, mine, :],
            send_sem=fw_send.at[n],
            recv_sem=fw_recv.at[n],
            device_id=(me, other),
            device_id_type=MESH,
        )

    def exchange(n):
        return pltpu.make_async_remote_copy(
            src_ref=part.at[n, :, theirs, :],
            dst_ref=got.at[n],
            send_sem=ex_send.at[n],
            recv_sem=ex_recv.at[n],
            device_id=(me, other),
            device_id_type=MESH,
        )

    def hand_over(n):
        return pltpu.make_async_remote_copy(
            src_ref=part.at[n],
            dst_ref=final_got.at[n - LATE],
            send_sem=ex_send.at[n],
            recv_sem=ex_recv.at[n],
            device_id=(me, chosen),
            device_id_type=MESH,
        )

    def give_last(n, i):
        target = chosen if i == 0 else 1 - chosen
        return pltpu.make_async_remote_copy(
            src_ref=final.at[n - LATE, :, pl.ds(pl.multiple_of(target * PROWS, PROWS), PROWS), :],
            dst_ref=kvgrad.at[:, :, pl.ds(pl.multiple_of(n * DIM, DIM), DIM)],
            send_sem=last_send.at[n - LATE, i],
            recv_sem=back_recv.at[n],
            device_id=(left, target),
            device_id_type=MESH,
        )

    def give_back(n):
        return pltpu.make_async_remote_copy(
            src_ref=back.at[n],
            dst_ref=kvgrad.at[:, :, pl.ds(pl.multiple_of(n * DIM, DIM), DIM)],
            send_sem=back_send.at[n],
            recv_sem=back_recv.at[n],
            device_id=(left, core),
            device_id_type=MESH,
        )

    pl.semaphore_wait(barrier, 2)

    @pl.when(tail == 1)
    def _():
        for copy in first_kv:
            copy.start()

    for copy in stage:
        copy.wait()

    @pl.when(tail == 0)
    def _():
        send_kv(0).start()

    for n in range(1, KV):
        send_kv(n).start()
    for copy in loads:
        copy.start()

    for copy in small:
        copy.wait()
    visible = offsets_s[left] < offsets_s[me]
    weight_row = jnp.zeros((1, RROWS), F32)
    for j in range(RESPONSES):
        weight_row = weight_row + jnp.where(ids_v[...] == j, adv_s[j], 0.0)
    square[...] = jnp.zeros_like(square)
    square[:, 0:RROWS] = jnp.broadcast_to(weight_row, (PROWS, RROWS))
    weight = square[...].T[0:RROWS, :]

    def turned(top, bottom):
        square[0:RROWS, 0:HEADS] = top
        square[RROWS:PROWS, 0:HEADS] = bottom
        return square[...].T

    def turned_response(values):
        return turned(values, jnp.concatenate((values[:, 4:], values[:, :4]), axis=1))

    lse_t = jnp.where(visible, lse_p[...] * LOG2E, HIDDEN)
    del_t = del_p[...]
    rlse_t = turned_response(lse_r[...]) * LOG2E
    rdel_t = turned_response(del_r[...] * weight[:, 0:HEADS])
    for n in range(KV):
        lp[n] = lse_t[n * PER : (n + 1) * PER]
        ep[n] = del_t[n * PER : (n + 1) * PER]
        lr[n] = rlse_t[n * PER : (n + 1) * PER]
        er[n] = rdel_t[n * PER : (n + 1) * PER]

    for copy in loads:
        copy.wait()

    def weigh(i, carry):
        columns = pl.ds(pl.multiple_of(i * DIM, DIM), DIM)
        w_r[:, columns] = (weight * c_r[:, columns].astype(F32)).astype(BF16)
        return carry

    lax.fori_loop(0, HEADS, weigh, 0)

    def spans(n, t):
        if t < 4:
            heads = (2 * t, 2 * t + 1)
        else:
            u = (t - 4) * 2
            heads = (u, u + 4, u + 1, u + 5)
        return [pl.ds(pl.multiple_of(n * PER * DIM + h * DIM, DIM), DIM) for h in heads]

    def rows_of(n, t, prompt, response):
        source = prompt if t < 4 else response
        return jnp.concatenate([source[:, columns] for columns in spans(n, t)], axis=0)

    def stats_of(n, t, prompt, response):
        source, first = (prompt, 2 * t) if t < 4 else (response, (t - 4) * 2)
        return jnp.concatenate((source[n, first : first + 1, :], source[n, first + 1 : first + 2, :]), axis=1)

    def scores(n, t, score):
        span = pl.ds(t * KEYS, KEYS)
        st = dot(kvin[n, 0], rows_of(n, t, q_p, q_r), 1, 1)
        gt = dot(kvin[n, 1], rows_of(n, t, c_p, w_r), 1, 1)
        p = jnp.exp2(st * SCALE2 - stats_of(n, t, lp, lr))
        probs[:, span] = p.astype(BF16)
        score[:, span] = (p * (gt - stats_of(n, t, ep, er))).astype(BF16)

    def query_grads(n, t, score):
        grad = dot(kvin[n, 0].T, score[:, pl.ds(t * KEYS, KEYS)], 1, 0)
        grad = (grad * SCALE).astype(BF16).T
        target, rows = (pgrad, PROWS) if t < 4 else (rgrad, RROWS)
        for i, columns in enumerate(spans(n, t)):
            target[:, columns] = grad[i * rows : (i + 1) * rows]

    def value_grads(n):
        cotangent = jnp.concatenate([rows_of(n, t, c_p, w_r) for t in range(TILES)], axis=0)
        part[n, 1] = dot(probs[...], cotangent, 1, 0).astype(BF16)

    def key_grads(n, score):
        queries = jnp.concatenate([rows_of(n, t, q_p, q_r) for t in range(TILES)], axis=0)
        part[n, 0] = (dot(score[...], queries, 1, 0) * SCALE).astype(BF16)

    def send_sum(n):
        exchange(n).wait_recv()
        back[n] = (part[n, :, mine, :].astype(F32) + got[n].astype(F32)).astype(BF16)
        give_back(n).start()

    def pass_on(n):
        late = n >= late_from

        @pl.when(jnp.logical_not(late))
        def _():
            exchange(n).start()

        @pl.when(jnp.logical_and(late, core != chosen))
        def _():
            hand_over(n).start()

    def combine(n):
        hand_over(n).wait_recv()
        final[n - LATE] = (part[n].astype(F32) + final_got[n - LATE].astype(F32)).astype(BF16)
        for i in range(2):
            give_last(n, i).start()

    def settle_late():
        @pl.when(lead == 0)
        def _():
            send_sum(LATE)

        @pl.when(jnp.logical_and(lead == 1, core == chosen))
        def _():
            combine(LATE)

    def settle_last():
        @pl.when(core == chosen)
        def _():
            combine(LAST)

    def step(n, score, before, first=False, last=False):
        if not (first or last):
            send_kv(n + 1).wait_recv()
            forward(n + 1).start()
        forward(n).wait_recv()
        for t in range(TILES):
            if first and t == TILES // 2:
                send_kv(n + 1).wait_recv()
                forward(n + 1).start()
            scores(n, t, score)
            if not first:
                query_grads(n - 1, t, before)
        value_grads(n)
        key_grads(n, score)
        if first:
            exchange(n).start()
        else:
            pass_on(n)
            if last:
                settle_late()
            else:
                send_sum(n - 1)

    send_kv(0).wait_recv()
    forward(0).start()
    step(0, score_a, score_b, first=True)

    def pair(m, carry):
        step(2 * m + 1, score_b, score_a)
        step(2 * m + 2, score_a, score_b)
        return carry

    lax.fori_loop(0, (KV - 2) // 2, pair, 0)
    step(KV - 1, score_b, score_a, last=True)
    for t in range(TILES):
        query_grads(KV - 1, t, score_b)
    settle_last()

    def finish(n, carry):
        @pl.when(n >= tail)
        def _():
            send_kv(n).wait_send()

        forward(n).wait_send()
        late = n >= late_from

        @pl.when(jnp.logical_not(late))
        def _():
            exchange(n).wait_send()
            give_back(n).wait_send()

        @pl.when(jnp.logical_and(late, core != chosen))
        def _():
            hand_over(n).wait_send()

        @pl.when(jnp.logical_and(late, core == chosen))
        def _():
            for i in range(2):
                give_last(n, i).wait_send()

        give_back(n).wait_recv()
        return carry


    @pl.when(tail == 1)
    def _():
        for copy in first_kv:
            copy.wait_send()

    lax.fori_loop(0, KV, finish, 0)


def write_out(rgrad, pgrad, kvgrad, rgrad_out, pgrad_out, kgrad_out, vgrad_out, sems):
    copies = [
        pltpu.make_async_copy(source, target, sems.at[i])
        for i, (source, target) in enumerate(
            (
                (pgrad, pgrad_out), (rgrad, rgrad_out),
                (kvgrad.at[0], kgrad_out), (kvgrad.at[1], vgrad_out),
            )
        )
    ]
    for copy in copies:
        copy.start()
    for copy in copies:
        copy.wait()


def body(pk, pv, offsets, pq, pc, plse, pdel, rq, rc, rlse, rdel, ids, adv):
    main = pl.BlockSpec(memory_space=pltpu.HBM)
    vector = pl.BlockSpec(memory_space=pltpu.VMEM)
    wide = HEADS * DIM
    operands = (pk, pv, offsets, pq, pc, plse.T, pdel.T, rq, rc, rlse, rdel, ids.reshape(1, RROWS), adv)
    operands = [pltpu.with_memory_space_constraint(x, pltpu.HBM) for x in operands]
    rgrad, pgrad, kvgrad = pl.pallas_call(
        kernel,
        out_shape=(
            pltpu.VMEM((RROWS, wide), BF16),
            pltpu.VMEM((PROWS, wide), BF16),
            pltpu.VMEM((2, PROWS, KV * DIM), BF16),
        ),
        in_specs=[main] * 13,
        out_specs=(vector, vector, vector),
        scratch_shapes=[
            pltpu.VMEM((2, PROWS, KV * DIM), BF16),
            pltpu.VMEM((KV, 2, KEYS, DIM), BF16),
            pltpu.VMEM((PROWS, wide), BF16),
            pltpu.VMEM((PROWS, wide), BF16),
            pltpu.VMEM((RROWS, wide), BF16),
            pltpu.VMEM((RROWS, wide), BF16),
            pltpu.VMEM((RROWS, wide), BF16),
            pltpu.VMEM((KV, PER, PROWS), F32),
            pltpu.VMEM((KV, PER, PROWS), F32),
            pltpu.VMEM((KV, PER, PROWS), F32),
            pltpu.VMEM((KV, PER, PROWS), F32),
            pltpu.VMEM((HEADS, PROWS), F32),
            pltpu.VMEM((HEADS, PROWS), F32),
            pltpu.VMEM((RROWS, HEADS), F32),
            pltpu.VMEM((RROWS, HEADS), F32),
            pltpu.VMEM((1, RROWS), jnp.int32),
            pltpu.SMEM(offsets.shape, jnp.int32),
            pltpu.SMEM((RESPONSES,), F32),
            pltpu.VMEM((PROWS, PROWS), F32),
            pltpu.VMEM((KEYS, TILES * KEYS), BF16),
            pltpu.VMEM((KEYS, TILES * KEYS), BF16),
            pltpu.VMEM((KEYS, TILES * KEYS), BF16),
            pltpu.VMEM((KV, 2, KEYS, DIM), BF16),
            pltpu.VMEM((KV, 2, PROWS, DIM), BF16),
            pltpu.VMEM((KV, 2, PROWS, DIM), BF16),
            pltpu.VMEM((2, 2, KEYS, DIM), BF16),
            pltpu.VMEM((2, 2, KEYS, DIM), BF16),
            pltpu.SemaphoreType.DMA((2,)),
            pltpu.SemaphoreType.DMA((2,)),
            pltpu.SemaphoreType.DMA((4,)),
            pltpu.SemaphoreType.DMA((7,)),
            pltpu.SemaphoreType.DMA((KV,)),
            pltpu.SemaphoreType.DMA((KV,)),
            pltpu.SemaphoreType.DMA((KV,)),
            pltpu.SemaphoreType.DMA((KV,)),
            pltpu.SemaphoreType.DMA((KV,)),
            pltpu.SemaphoreType.DMA((KV,)),
            pltpu.SemaphoreType.DMA((KV,)),
            pltpu.SemaphoreType.DMA((KV,)),
            pltpu.SemaphoreType.DMA((2, 2)),
        ],
        compiler_params=pltpu.CompilerParams(
            collective_id=0, has_side_effects=True, vmem_limit_bytes=28 * 2**20
        ),
        name="prefix_backward",
    )(*operands)
    grads = [pltpu.with_memory_space_constraint(x, pltpu.VMEM) for x in (rgrad, pgrad, kvgrad)]
    return pl.pallas_call(
        write_out,
        out_shape=(
            jax.ShapeDtypeStruct((RROWS, wide), BF16),
            jax.ShapeDtypeStruct((PROWS, wide), BF16),
            jax.ShapeDtypeStruct((PROWS, KV * DIM), BF16),
            jax.ShapeDtypeStruct((PROWS, KV * DIM), BF16),
        ),
        in_specs=[vector] * 3,
        out_specs=(main, main, main, main),
        scratch_shapes=[pltpu.SemaphoreType.DMA((4,))],
        compiler_params=pltpu.CompilerParams(vmem_limit_bytes=4 * 2**20),
        name="write_out",
    )(*grads)


def solution(mesh):
    rows = P(("ctx", "rsp"), None)
    return jax.shard_map(
        body,
        mesh=mesh,
        in_specs=(rows, rows, P(), rows, rows, rows, rows, rows, rows, rows, rows, P(("ctx", "rsp")), P()),
        out_specs=(rows, rows, rows, rows),
        check_vma=False,
    )
```

```python
import jax
import jax.numpy as jnp
from jax import lax
from jax.experimental import pallas as pl
from jax.experimental.pallas import tpu as pltpu
from jax.sharding import PartitionSpec as P

HEADS = 64
KV = 8
PER = HEADS // KV
LATE = KV - 2
LAST = KV - 1
DIM = 128
RESPONSES = 16
PROWS = 128
RROWS = 64
KEYS = 256
TILES = 6
SCALE = float(DIM**-0.5)
LOG2E = 1.4426950408889634
SCALE2 = SCALE * LOG2E
HIDDEN = 1e30
F32 = jnp.float32
BF16 = jnp.bfloat16
MESH = pl.DeviceIdType.MESH


def dot(a, b, ca, cb):
    return lax.dot_general(a, b, (((ca,), (cb,)), ((), ())), preferred_element_type=F32)


def kernel(
    pk, pv, offsets, pq, pc, plse, pdel, rq, rc, rlse, rdel, ids, adv,
    rgrad, pgrad, kvgrad,
    kvsrc, kvin, q_p, c_p, q_r, c_r, w_r,
    lp, ep, lr, er, lse_p, del_p, lse_r, del_r, ids_v, offsets_s, adv_s, square,
    probs, score_a, score_b, part, got, back, final, final_got,
    first_send, stage_sem, load_sem, small_sem, kv_send, kv_recv, fw_send, fw_recv,
    ex_send, ex_recv, back_send, back_recv, last_send,
):
    count = lax.axis_size("ctx")
    me = lax.axis_index("ctx")
    core = lax.axis_index("rsp")
    right = lax.rem(me + 1, count)
    left = lax.rem(me + count - 1, count)
    other = 1 - core
    lead = (count - 1 - me) // (count - 1)
    tail = me // (count - 1)
    chosen = 1 - lead
    late_from = KV - 1 - lead
    mine = pl.ds(pl.multiple_of(core * PROWS, PROWS), PROWS)
    theirs = pl.ds(pl.multiple_of(other * PROWS, PROWS), PROWS)

    barrier = pltpu.get_barrier_semaphore()
    for device in ((left, core), (me, other)):
        pl.semaphore_signal(barrier, inc=1, device_id=device, device_id_type=MESH)

    small = [
        pltpu.make_async_copy(source, target, small_sem.at[i])
        for i, (source, target) in enumerate(
            (
                (ids, ids_v), (plse, lse_p), (pdel, del_p), (rlse, lse_r),
                (rdel, del_r), (offsets, offsets_s), (adv, adv_s),
            )
        )
    ]
    loads = [
        pltpu.make_async_copy(source, target, load_sem.at[i])
        for i, (source, target) in enumerate(((rc, c_r), (pq, q_p), (pc, c_p), (rq, q_r)))
    ]
    stage = [pltpu.make_async_copy(source, kvsrc.at[i], stage_sem.at[i]) for i, source in enumerate((pk, pv))]
    for copy in stage + small:
        copy.start()

    def send_kv(n):
        return pltpu.make_async_remote_copy(
            src_ref=kvsrc.at[:, :, pl.ds(pl.multiple_of(n * DIM, DIM), DIM)],
            dst_ref=kvin.at[n, :, mine, :],
            send_sem=kv_send.at[n],
            recv_sem=kv_recv.at[n],
            device_id=(right, core),
            device_id_type=MESH,
        )

    first_kv = [
        pltpu.make_async_remote_copy(
            src_ref=source.at[:, pl.ds(0, DIM)],
            dst_ref=kvin.at[0, i, mine, :],
            send_sem=first_send.at[i],
            recv_sem=kv_recv.at[0],
            device_id=(right, core),
            device_id_type=MESH,
        )
        for i, source in enumerate((pk, pv))
    ]

    def forward(n):
        return pltpu.make_async_remote_copy(
            src_ref=kvin.at[n, :, mine, :],
            dst_ref=kvin.at[n, :, mine, :],
            send_sem=fw_send.at[n],
            recv_sem=fw_recv.at[n],
            device_id=(me, other),
            device_id_type=MESH,
        )

    def exchange(n):
        return pltpu.make_async_remote_copy(
            src_ref=part.at[n, :, theirs, :],
            dst_ref=got.at[n],
            send_sem=ex_send.at[n],
            recv_sem=ex_recv.at[n],
            device_id=(me, other),
            device_id_type=MESH,
        )

    def hand_over(n):
        return pltpu.make_async_remote_copy(
            src_ref=part.at[n],
            dst_ref=final_got.at[n - LATE],
            send_sem=ex_send.at[n],
            recv_sem=ex_recv.at[n],
            device_id=(me, chosen),
            device_id_type=MESH,
        )

    def give_last(n, i):
        target = chosen if i == 0 else 1 - chosen
        return pltpu.make_async_remote_copy(
            src_ref=final.at[n - LATE, :, pl.ds(pl.multiple_of(target * PROWS, PROWS), PROWS), :],
            dst_ref=kvgrad.at[:, :, pl.ds(pl.multiple_of(n * DIM, DIM), DIM)],
            send_sem=last_send.at[n - LATE, i],
            recv_sem=back_recv.at[n],
            device_id=(left, target),
            device_id_type=MESH,
        )

    def give_back(n):
        return pltpu.make_async_remote_copy(
            src_ref=back.at[n],
            dst_ref=kvgrad.at[:, :, pl.ds(pl.multiple_of(n * DIM, DIM), DIM)],
            send_sem=back_send.at[n],
            recv_sem=back_recv.at[n],
            device_id=(left, core),
            device_id_type=MESH,
        )

    pl.semaphore_wait(barrier, 2)

    @pl.when(tail == 1)
    def _():
        for copy in first_kv:
            copy.start()

    for copy in stage:
        copy.wait()

    @pl.when(tail == 0)
    def _():
        send_kv(0).start()

    for n in range(1, KV):
        send_kv(n).start()
    for copy in loads:
        copy.start()

    for copy in small:
        copy.wait()
    visible = offsets_s[left] < offsets_s[me]
    weight_row = jnp.zeros((1, RROWS), F32)
    for j in range(RESPONSES):
        weight_row = weight_row + jnp.where(ids_v[...] == j, adv_s[j], 0.0)
    square[...] = jnp.zeros_like(square)
    square[:, 0:RROWS] = jnp.broadcast_to(weight_row, (PROWS, RROWS))
    weight = square[...].T[0:RROWS, :]

    def turned(top, bottom):
        square[0:RROWS, 0:HEADS] = top
        square[RROWS:PROWS, 0:HEADS] = bottom
        return square[...].T

    def turned_response(values):
        return turned(values, jnp.concatenate((values[:, 4:], values[:, :4]), axis=1))

    lse_t = jnp.where(visible, lse_p[...] * LOG2E, HIDDEN)
    del_t = del_p[...]
    rlse_t = turned_response(lse_r[...]) * LOG2E
    rdel_t = turned_response(del_r[...] * weight[:, 0:HEADS])
    for n in range(KV):
        lp[n] = lse_t[n * PER : (n + 1) * PER]
        ep[n] = del_t[n * PER : (n + 1) * PER]
        lr[n] = rlse_t[n * PER : (n + 1) * PER]
        er[n] = rdel_t[n * PER : (n + 1) * PER]

    for copy in loads:
        copy.wait()

    def weigh(i, carry):
        columns = pl.ds(pl.multiple_of(i * DIM, DIM), DIM)
        w_r[:, columns] = (weight * c_r[:, columns].astype(F32)).astype(BF16)
        return carry

    lax.fori_loop(0, HEADS, weigh, 0)

    def spans(n, t):
        if t < 4:
            heads = (2 * t, 2 * t + 1)
        else:
            u = (t - 4) * 2
            heads = (u, u + 4, u + 1, u + 5)
        return [pl.ds(pl.multiple_of(n * PER * DIM + h * DIM, DIM), DIM) for h in heads]

    def rows_of(n, t, prompt, response):
        source = prompt if t < 4 else response
        return jnp.concatenate([source[:, columns] for columns in spans(n, t)], axis=0)

    def stats_of(n, t, prompt, response):
        source, first = (prompt, 2 * t) if t < 4 else (response, (t - 4) * 2)
        return jnp.concatenate((source[n, first : first + 1, :], source[n, first + 1 : first + 2, :]), axis=1)

    def scores(n, t, score):
        span = pl.ds(t * KEYS, KEYS)
        st = dot(kvin[n, 0], rows_of(n, t, q_p, q_r), 1, 1)
        gt = dot(kvin[n, 1], rows_of(n, t, c_p, w_r), 1, 1)
        p = jnp.exp2(st * SCALE2 - stats_of(n, t, lp, lr))
        probs[:, span] = p.astype(BF16)
        score[:, span] = (p * (gt - stats_of(n, t, ep, er))).astype(BF16)

    def query_grads(n, t, score):
        grad = dot(kvin[n, 0].T, score[:, pl.ds(t * KEYS, KEYS)], 1, 0)
        grad = (grad * SCALE).astype(BF16).T
        target, rows = (pgrad, PROWS) if t < 4 else (rgrad, RROWS)
        for i, columns in enumerate(spans(n, t)):
            target[:, columns] = grad[i * rows : (i + 1) * rows]

    def value_grads(n):
        cotangent = jnp.concatenate([rows_of(n, t, c_p, w_r) for t in range(TILES)], axis=0)
        part[n, 1] = dot(probs[...], cotangent, 1, 0).astype(BF16)

    def key_grads(n, score):
        queries = jnp.concatenate([rows_of(n, t, q_p, q_r) for t in range(TILES)], axis=0)
        part[n, 0] = (dot(score[...], queries, 1, 0) * SCALE).astype(BF16)

    def send_sum(n):
        exchange(n).wait_recv()
        back[n] = (part[n, :, mine, :].astype(F32) + got[n].astype(F32)).astype(BF16)
        give_back(n).start()

    def pass_on(n):
        late = n >= late_from

        @pl.when(jnp.logical_not(late))
        def _():
            exchange(n).start()

        @pl.when(jnp.logical_and(late, core != chosen))
        def _():
            hand_over(n).start()

    def combine(n):
        hand_over(n).wait_recv()
        final[n - LATE] = (part[n].astype(F32) + final_got[n - LATE].astype(F32)).astype(BF16)
        for i in range(2):
            give_last(n, i).start()

    def settle_late():
        @pl.when(lead == 0)
        def _():
            send_sum(LATE)

        @pl.when(jnp.logical_and(lead == 1, core == chosen))
        def _():
            combine(LATE)

    def settle_last():
        @pl.when(core == chosen)
        def _():
            combine(LAST)

    def step(n, score, before, first=False, last=False):
        if not (first or last):
            send_kv(n + 1).wait_recv()
            forward(n + 1).start()
        forward(n).wait_recv()
        for t in range(TILES):
            if first and t == TILES // 2:
                send_kv(n + 1).wait_recv()
                forward(n + 1).start()
            scores(n, t, score)
        value_grads(n)
        if not first:
            for t in range(TILES):
                query_grads(n - 1, t, before)
        key_grads(n, score)
        if first:
            exchange(n).start()
        else:
            pass_on(n)
            if last:
                settle_late()
            else:
                send_sum(n - 1)

    send_kv(0).wait_recv()
    forward(0).start()
    step(0, score_a, score_b, first=True)

    def pair(m, carry):
        step(2 * m + 1, score_b, score_a)
        step(2 * m + 2, score_a, score_b)
        return carry

    lax.fori_loop(0, (KV - 2) // 2, pair, 0)
    step(KV - 1, score_b, score_a, last=True)
    for t in range(TILES):
        query_grads(KV - 1, t, score_b)
    settle_last()

    def finish(n, carry):
        @pl.when(n >= tail)
        def _():
            send_kv(n).wait_send()

        forward(n).wait_send()
        late = n >= late_from

        @pl.when(jnp.logical_not(late))
        def _():
            exchange(n).wait_send()
            give_back(n).wait_send()

        @pl.when(jnp.logical_and(late, core != chosen))
        def _():
            hand_over(n).wait_send()

        @pl.when(jnp.logical_and(late, core == chosen))
        def _():
            for i in range(2):
                give_last(n, i).wait_send()

        give_back(n).wait_recv()
        return carry


    @pl.when(tail == 1)
    def _():
        for copy in first_kv:
            copy.wait_send()

    lax.fori_loop(0, KV, finish, 0)


def write_out(rgrad, pgrad, kvgrad, rgrad_out, pgrad_out, kgrad_out, vgrad_out, sems):
    copies = [
        pltpu.make_async_copy(source, target, sems.at[i])
        for i, (source, target) in enumerate(
            (
                (pgrad, pgrad_out), (rgrad, rgrad_out),
                (kvgrad.at[0], kgrad_out), (kvgrad.at[1], vgrad_out),
            )
        )
    ]
    for copy in copies:
        copy.start()
    for copy in copies:
        copy.wait()


def body(pk, pv, offsets, pq, pc, plse, pdel, rq, rc, rlse, rdel, ids, adv):
    main = pl.BlockSpec(memory_space=pltpu.HBM)
    vector = pl.BlockSpec(memory_space=pltpu.VMEM)
    wide = HEADS * DIM
    operands = (pk, pv, offsets, pq, pc, plse.T, pdel.T, rq, rc, rlse, rdel, ids.reshape(1, RROWS), adv)
    operands = [pltpu.with_memory_space_constraint(x, pltpu.HBM) for x in operands]
    rgrad, pgrad, kvgrad = pl.pallas_call(
        kernel,
        out_shape=(
            pltpu.VMEM((RROWS, wide), BF16),
            pltpu.VMEM((PROWS, wide), BF16),
            pltpu.VMEM((2, PROWS, KV * DIM), BF16),
        ),
        in_specs=[main] * 13,
        out_specs=(vector, vector, vector),
        scratch_shapes=[
            pltpu.VMEM((2, PROWS, KV * DIM), BF16),
            pltpu.VMEM((KV, 2, KEYS, DIM), BF16),
            pltpu.VMEM((PROWS, wide), BF16),
            pltpu.VMEM((PROWS, wide), BF16),
            pltpu.VMEM((RROWS, wide), BF16),
            pltpu.VMEM((RROWS, wide), BF16),
            pltpu.VMEM((RROWS, wide), BF16),
            pltpu.VMEM((KV, PER, PROWS), F32),
            pltpu.VMEM((KV, PER, PROWS), F32),
            pltpu.VMEM((KV, PER, PROWS), F32),
            pltpu.VMEM((KV, PER, PROWS), F32),
            pltpu.VMEM((HEADS, PROWS), F32),
            pltpu.VMEM((HEADS, PROWS), F32),
            pltpu.VMEM((RROWS, HEADS), F32),
            pltpu.VMEM((RROWS, HEADS), F32),
            pltpu.VMEM((1, RROWS), jnp.int32),
            pltpu.SMEM(offsets.shape, jnp.int32),
            pltpu.SMEM((RESPONSES,), F32),
            pltpu.VMEM((PROWS, PROWS), F32),
            pltpu.VMEM((KEYS, TILES * KEYS), BF16),
            pltpu.VMEM((KEYS, TILES * KEYS), BF16),
            pltpu.VMEM((KEYS, TILES * KEYS), BF16),
            pltpu.VMEM((KV, 2, KEYS, DIM), BF16),
            pltpu.VMEM((KV, 2, PROWS, DIM), BF16),
            pltpu.VMEM((KV, 2, PROWS, DIM), BF16),
            pltpu.VMEM((2, 2, KEYS, DIM), BF16),
            pltpu.VMEM((2, 2, KEYS, DIM), BF16),
            pltpu.SemaphoreType.DMA((2,)),
            pltpu.SemaphoreType.DMA((2,)),
            pltpu.SemaphoreType.DMA((4,)),
            pltpu.SemaphoreType.DMA((7,)),
            pltpu.SemaphoreType.DMA((KV,)),
            pltpu.SemaphoreType.DMA((KV,)),
            pltpu.SemaphoreType.DMA((KV,)),
            pltpu.SemaphoreType.DMA((KV,)),
            pltpu.SemaphoreType.DMA((KV,)),
            pltpu.SemaphoreType.DMA((KV,)),
            pltpu.SemaphoreType.DMA((KV,)),
            pltpu.SemaphoreType.DMA((KV,)),
            pltpu.SemaphoreType.DMA((2, 2)),
        ],
        compiler_params=pltpu.CompilerParams(
            collective_id=0, has_side_effects=True, vmem_limit_bytes=28 * 2**20
        ),
        name="prefix_backward",
    )(*operands)
    grads = [pltpu.with_memory_space_constraint(x, pltpu.VMEM) for x in (rgrad, pgrad, kvgrad)]
    return pl.pallas_call(
        write_out,
        out_shape=(
            jax.ShapeDtypeStruct((RROWS, wide), BF16),
            jax.ShapeDtypeStruct((PROWS, wide), BF16),
            jax.ShapeDtypeStruct((PROWS, KV * DIM), BF16),
            jax.ShapeDtypeStruct((PROWS, KV * DIM), BF16),
        ),
        in_specs=[vector] * 3,
        out_specs=(main, main, main, main),
        scratch_shapes=[pltpu.SemaphoreType.DMA((4,))],
        compiler_params=pltpu.CompilerParams(vmem_limit_bytes=4 * 2**20),
        name="write_out",
    )(*grads)


def solution(mesh):
    rows = P(("ctx", "rsp"), None)
    return jax.shard_map(
        body,
        mesh=mesh,
        in_specs=(rows, rows, P(), rows, rows, rows, rows, rows, rows, rows, rows, P(("ctx", "rsp")), P()),
        out_specs=(rows, rows, rows, rows),
        check_vma=False,
    )
```

```python
import jax
import jax.numpy as jnp
from jax import lax
from jax.experimental import pallas as pl
from jax.experimental.pallas import tpu as pltpu
from jax.sharding import PartitionSpec as P

HEADS = 64
KV = 8
PER = HEADS // KV
LATE = KV - 2
LAST = KV - 1
DIM = 128
RESPONSES = 16
PROWS = 128
RROWS = 64
KEYS = 256
TILES = 6
SCALE = float(DIM**-0.5)
LOG2E = 1.4426950408889634
SCALE2 = SCALE * LOG2E
HIDDEN = 1e30
F32 = jnp.float32
BF16 = jnp.bfloat16
MESH = pl.DeviceIdType.MESH


def dot(a, b, ca, cb):
    return lax.dot_general(a, b, (((ca,), (cb,)), ((), ())), preferred_element_type=F32)


def kernel(
    pk, pv, offsets, pq, pc, plse, pdel, rq, rc, rlse, rdel, ids, adv,
    rgrad, pgrad, kvgrad,
    kvsrc, kvin, q_p, c_p, q_r, c_r, w_r,
    lp, ep, lr, er, lse_p, del_p, lse_r, del_r, ids_v, offsets_s, adv_s, square,
    probs, score_a, score_b, part, got, back, final, final_got,
    first_send, stage_sem, load_sem, small_sem, kv_send, kv_recv, fw_send, fw_recv,
    ex_send, ex_recv, back_send, back_recv, last_send,
):
    count = lax.axis_size("ctx")
    me = lax.axis_index("ctx")
    core = lax.axis_index("rsp")
    left = lax.rem(me + count - 1, count)
    other = 1 - core

    barrier = pltpu.get_barrier_semaphore()
    for device in ((left, core), (me, other)):
        pl.semaphore_signal(barrier, inc=1, device_id=device, device_id_type=MESH)

    small = [
        pltpu.make_async_copy(source, target, small_sem.at[i])
        for i, (source, target) in enumerate(
            (
                (ids, ids_v), (plse, lse_p), (pdel, del_p), (rlse, lse_r),
                (rdel, del_r), (offsets, offsets_s), (adv, adv_s),
            )
        )
    ]
    loads = [
        pltpu.make_async_copy(source, target, load_sem.at[i])
        for i, (source, target) in enumerate(((rc, c_r), (pq, q_p), (pc, c_p), (rq, q_r)))
    ]
    right = lax.rem(me + 1, count)
    lead = (count - 1 - me) // (count - 1)
    tail = me // (count - 1)
    chosen = 1 - lead
    late_from = KV - 1 - lead
    mine = pl.ds(pl.multiple_of(core * PROWS, PROWS), PROWS)
    theirs = pl.ds(pl.multiple_of(other * PROWS, PROWS), PROWS)

    stage = [pltpu.make_async_copy(source, kvsrc.at[i], stage_sem.at[i]) for i, source in enumerate((pk, pv))]
    for copy in stage + small:
        copy.start()

    def send_kv(n):
        return pltpu.make_async_remote_copy(
            src_ref=kvsrc.at[:, :, pl.ds(pl.multiple_of(n * DIM, DIM), DIM)],
            dst_ref=kvin.at[n, :, mine, :],
            send_sem=kv_send.at[n],
            recv_sem=kv_recv.at[n],
            device_id=(right, core),
            device_id_type=MESH,
        )

    first_kv = [
        pltpu.make_async_remote_copy(
            src_ref=source.at[:, pl.ds(0, DIM)],
            dst_ref=kvin.at[0, i, mine, :],
            send_sem=first_send.at[i],
            recv_sem=kv_recv.at[0],
            device_id=(right, core),
            device_id_type=MESH,
        )
        for i, source in enumerate((pk, pv))
    ]

    def forward(n):
        return pltpu.make_async_remote_copy(
            src_ref=kvin.at[n, :, mine, :],
            dst_ref=kvin.at[n, :, mine, :],
            send_sem=fw_send.at[n],
            recv_sem=fw_recv.at[n],
            device_id=(me, other),
            device_id_type=MESH,
        )

    def exchange(n):
        return pltpu.make_async_remote_copy(
            src_ref=part.at[n, :, theirs, :],
            dst_ref=got.at[n],
            send_sem=ex_send.at[n],
            recv_sem=ex_recv.at[n],
            device_id=(me, other),
            device_id_type=MESH,
        )

    def hand_over(n):
        return pltpu.make_async_remote_copy(
            src_ref=part.at[n],
            dst_ref=final_got.at[n - LATE],
            send_sem=ex_send.at[n],
            recv_sem=ex_recv.at[n],
            device_id=(me, chosen),
            device_id_type=MESH,
        )

    def give_last(n, i):
        target = chosen if i == 0 else 1 - chosen
        return pltpu.make_async_remote_copy(
            src_ref=final.at[n - LATE, :, pl.ds(pl.multiple_of(target * PROWS, PROWS), PROWS), :],
            dst_ref=kvgrad.at[:, :, pl.ds(pl.multiple_of(n * DIM, DIM), DIM)],
            send_sem=last_send.at[n - LATE, i],
            recv_sem=back_recv.at[n],
            device_id=(left, target),
            device_id_type=MESH,
        )

    def give_back(n):
        return pltpu.make_async_remote_copy(
            src_ref=back.at[n],
            dst_ref=kvgrad.at[:, :, pl.ds(pl.multiple_of(n * DIM, DIM), DIM)],
            send_sem=back_send.at[n],
            recv_sem=back_recv.at[n],
            device_id=(left, core),
            device_id_type=MESH,
        )

    pl.semaphore_wait(barrier, 2)

    @pl.when(tail == 1)
    def _():
        for copy in first_kv:
            copy.start()

    for copy in stage:
        copy.wait()

    @pl.when(tail == 0)
    def _():
        send_kv(0).start()

    for n in range(1, KV):
        send_kv(n).start()
    for copy in loads:
        copy.start()

    for copy in small:
        copy.wait()
    visible = offsets_s[left] < offsets_s[me]
    weight_row = jnp.zeros((1, RROWS), F32)
    for j in range(RESPONSES):
        weight_row = weight_row + jnp.where(ids_v[...] == j, adv_s[j], 0.0)
    square[...] = jnp.zeros_like(square)
    square[:, 0:RROWS] = jnp.broadcast_to(weight_row, (PROWS, RROWS))
    weight = square[...].T[0:RROWS, :]

    def turned(top, bottom):
        square[0:RROWS, 0:HEADS] = top
        square[RROWS:PROWS, 0:HEADS] = bottom
        return square[...].T

    def turned_response(values):
        return turned(values, jnp.concatenate((values[:, 4:], values[:, :4]), axis=1))

    lse_t = jnp.where(visible, lse_p[...] * LOG2E, HIDDEN)
    del_t = del_p[...]
    rlse_t = turned_response(lse_r[...]) * LOG2E
    rdel_t = turned_response(del_r[...] * weight[:, 0:HEADS])
    for n in range(KV):
        lp[n] = lse_t[n * PER : (n + 1) * PER]
        ep[n] = del_t[n * PER : (n + 1) * PER]
        lr[n] = rlse_t[n * PER : (n + 1) * PER]
        er[n] = rdel_t[n * PER : (n + 1) * PER]

    for copy in loads:
        copy.wait()

    def weigh(i, carry):
        columns = pl.ds(pl.multiple_of(i * DIM, DIM), DIM)
        w_r[:, columns] = (weight * c_r[:, columns].astype(F32)).astype(BF16)
        return carry

    lax.fori_loop(0, HEADS, weigh, 0)

    def spans(n, t):
        if t < 4:
            heads = (2 * t, 2 * t + 1)
        else:
            u = (t - 4) * 2
            heads = (u, u + 4, u + 1, u + 5)
        return [pl.ds(pl.multiple_of(n * PER * DIM + h * DIM, DIM), DIM) for h in heads]

    def rows_of(n, t, prompt, response):
        source = prompt if t < 4 else response
        return jnp.concatenate([source[:, columns] for columns in spans(n, t)], axis=0)

    def stats_of(n, t, prompt, response):
        source, first = (prompt, 2 * t) if t < 4 else (response, (t - 4) * 2)
        return jnp.concatenate((source[n, first : first + 1, :], source[n, first + 1 : first + 2, :]), axis=1)

    def scores(n, t, score):
        span = pl.ds(t * KEYS, KEYS)
        st = dot(kvin[n, 0], rows_of(n, t, q_p, q_r), 1, 1)
        gt = dot(kvin[n, 1], rows_of(n, t, c_p, w_r), 1, 1)
        p = jnp.exp2(st * SCALE2 - stats_of(n, t, lp, lr))
        probs[:, span] = p.astype(BF16)
        score[:, span] = (p * (gt - stats_of(n, t, ep, er))).astype(BF16)

    def query_grads(n, t, score):
        grad = dot(kvin[n, 0].T, score[:, pl.ds(t * KEYS, KEYS)], 1, 0)
        grad = (grad * SCALE).astype(BF16).T
        target, rows = (pgrad, PROWS) if t < 4 else (rgrad, RROWS)
        for i, columns in enumerate(spans(n, t)):
            target[:, columns] = grad[i * rows : (i + 1) * rows]

    def value_grads(n):
        cotangent = jnp.concatenate([rows_of(n, t, c_p, w_r) for t in range(TILES)], axis=0)
        part[n, 1] = dot(probs[...], cotangent, 1, 0).astype(BF16)

    def key_grads(n, score):
        queries = jnp.concatenate([rows_of(n, t, q_p, q_r) for t in range(TILES)], axis=0)
        part[n, 0] = (dot(score[...], queries, 1, 0) * SCALE).astype(BF16)

    def send_sum(n):
        exchange(n).wait_recv()
        back[n] = (part[n, :, mine, :].astype(F32) + got[n].astype(F32)).astype(BF16)
        give_back(n).start()

    def pass_on(n):
        late = n >= late_from

        @pl.when(jnp.logical_not(late))
        def _():
            exchange(n).start()

        @pl.when(jnp.logical_and(late, core != chosen))
        def _():
            hand_over(n).start()

    def combine(n):
        hand_over(n).wait_recv()
        final[n - LATE] = (part[n].astype(F32) + final_got[n - LATE].astype(F32)).astype(BF16)
        for i in range(2):
            give_last(n, i).start()

    def settle_late():
        @pl.when(lead == 0)
        def _():
            send_sum(LATE)

        @pl.when(jnp.logical_and(lead == 1, core == chosen))
        def _():
            combine(LATE)

    def settle_last():
        @pl.when(core == chosen)
        def _():
            combine(LAST)

    def step(n, score, before, first=False, last=False):
        if not (first or last):
            send_kv(n + 1).wait_recv()
            forward(n + 1).start()
        forward(n).wait_recv()
        for t in range(TILES):
            if first and t == TILES // 2:
                send_kv(n + 1).wait_recv()
                forward(n + 1).start()
            scores(n, t, score)
        value_grads(n)
        if not first:
            for t in range(TILES):
                query_grads(n - 1, t, before)
        key_grads(n, score)
        if first:
            exchange(n).start()
        else:
            pass_on(n)
            if last:
                settle_late()
            else:
                send_sum(n - 1)

    send_kv(0).wait_recv()
    forward(0).start()
    step(0, score_a, score_b, first=True)

    def pair(m, carry):
        step(2 * m + 1, score_b, score_a)
        step(2 * m + 2, score_a, score_b)
        return carry

    lax.fori_loop(0, (KV - 2) // 2, pair, 0)
    step(KV - 1, score_b, score_a, last=True)
    for t in range(TILES):
        query_grads(KV - 1, t, score_b)
    settle_last()

    def finish(n, carry):
        @pl.when(n >= tail)
        def _():
            send_kv(n).wait_send()

        forward(n).wait_send()
        late = n >= late_from

        @pl.when(jnp.logical_not(late))
        def _():
            exchange(n).wait_send()
            give_back(n).wait_send()

        @pl.when(jnp.logical_and(late, core != chosen))
        def _():
            hand_over(n).wait_send()

        @pl.when(jnp.logical_and(late, core == chosen))
        def _():
            for i in range(2):
                give_last(n, i).wait_send()

        give_back(n).wait_recv()
        return carry


    @pl.when(tail == 1)
    def _():
        for copy in first_kv:
            copy.wait_send()

    lax.fori_loop(0, KV, finish, 0)


def write_out(rgrad, pgrad, kvgrad, rgrad_out, pgrad_out, kgrad_out, vgrad_out, sems):
    copies = [
        pltpu.make_async_copy(source, target, sems.at[i])
        for i, (source, target) in enumerate(
            (
                (pgrad, pgrad_out), (rgrad, rgrad_out),
                (kvgrad.at[0], kgrad_out), (kvgrad.at[1], vgrad_out),
            )
        )
    ]
    for copy in copies:
        copy.start()
    for copy in copies:
        copy.wait()


def body(pk, pv, offsets, pq, pc, plse, pdel, rq, rc, rlse, rdel, ids, adv):
    main = pl.BlockSpec(memory_space=pltpu.HBM)
    vector = pl.BlockSpec(memory_space=pltpu.VMEM)
    wide = HEADS * DIM
    operands = (pk, pv, offsets, pq, pc, plse.T, pdel.T, rq, rc, rlse, rdel, ids.reshape(1, RROWS), adv)
    operands = [pltpu.with_memory_space_constraint(x, pltpu.HBM) for x in operands]
    rgrad, pgrad, kvgrad = pl.pallas_call(
        kernel,
        out_shape=(
            pltpu.VMEM((RROWS, wide), BF16),
            pltpu.VMEM((PROWS, wide), BF16),
            pltpu.VMEM((2, PROWS, KV * DIM), BF16),
        ),
        in_specs=[main] * 13,
        out_specs=(vector, vector, vector),
        scratch_shapes=[
            pltpu.VMEM((2, PROWS, KV * DIM), BF16),
            pltpu.VMEM((KV, 2, KEYS, DIM), BF16),
            pltpu.VMEM((PROWS, wide), BF16),
            pltpu.VMEM((PROWS, wide), BF16),
            pltpu.VMEM((RROWS, wide), BF16),
            pltpu.VMEM((RROWS, wide), BF16),
            pltpu.VMEM((RROWS, wide), BF16),
            pltpu.VMEM((KV, PER, PROWS), F32),
            pltpu.VMEM((KV, PER, PROWS), F32),
            pltpu.VMEM((KV, PER, PROWS), F32),
            pltpu.VMEM((KV, PER, PROWS), F32),
            pltpu.VMEM((HEADS, PROWS), F32),
            pltpu.VMEM((HEADS, PROWS), F32),
            pltpu.VMEM((RROWS, HEADS), F32),
            pltpu.VMEM((RROWS, HEADS), F32),
            pltpu.VMEM((1, RROWS), jnp.int32),
            pltpu.SMEM(offsets.shape, jnp.int32),
            pltpu.SMEM((RESPONSES,), F32),
            pltpu.VMEM((PROWS, PROWS), F32),
            pltpu.VMEM((KEYS, TILES * KEYS), BF16),
            pltpu.VMEM((KEYS, TILES * KEYS), BF16),
            pltpu.VMEM((KEYS, TILES * KEYS), BF16),
            pltpu.VMEM((KV, 2, KEYS, DIM), BF16),
            pltpu.VMEM((KV, 2, PROWS, DIM), BF16),
            pltpu.VMEM((KV, 2, PROWS, DIM), BF16),
            pltpu.VMEM((2, 2, KEYS, DIM), BF16),
            pltpu.VMEM((2, 2, KEYS, DIM), BF16),
            pltpu.SemaphoreType.DMA((2,)),
            pltpu.SemaphoreType.DMA((2,)),
            pltpu.SemaphoreType.DMA((4,)),
            pltpu.SemaphoreType.DMA((7,)),
            pltpu.SemaphoreType.DMA((KV,)),
            pltpu.SemaphoreType.DMA((KV,)),
            pltpu.SemaphoreType.DMA((KV,)),
            pltpu.SemaphoreType.DMA((KV,)),
            pltpu.SemaphoreType.DMA((KV,)),
            pltpu.SemaphoreType.DMA((KV,)),
            pltpu.SemaphoreType.DMA((KV,)),
            pltpu.SemaphoreType.DMA((KV,)),
            pltpu.SemaphoreType.DMA((2, 2)),
        ],
        compiler_params=pltpu.CompilerParams(
            collective_id=0, has_side_effects=True, vmem_limit_bytes=28 * 2**20
        ),
        name="prefix_backward",
    )(*operands)
    grads = [pltpu.with_memory_space_constraint(x, pltpu.VMEM) for x in (rgrad, pgrad, kvgrad)]
    return pl.pallas_call(
        write_out,
        out_shape=(
            jax.ShapeDtypeStruct((RROWS, wide), BF16),
            jax.ShapeDtypeStruct((PROWS, wide), BF16),
            jax.ShapeDtypeStruct((PROWS, KV * DIM), BF16),
            jax.ShapeDtypeStruct((PROWS, KV * DIM), BF16),
        ),
        in_specs=[vector] * 3,
        out_specs=(main, main, main, main),
        scratch_shapes=[pltpu.SemaphoreType.DMA((4,))],
        compiler_params=pltpu.CompilerParams(vmem_limit_bytes=4 * 2**20),
        name="write_out",
    )(*grads)


def solution(mesh):
    rows = P(("ctx", "rsp"), None)
    return jax.shard_map(
        body,
        mesh=mesh,
        in_specs=(rows, rows, P(), rows, rows, rows, rows, rows, rows, rows, rows, P(("ctx", "rsp")), P()),
        out_specs=(rows, rows, rows, rows),
        check_vma=False,
    )
```
